32 devices in a mesh: mem: 4 (over z), grid: 8 (over y, x, core).
Axes of the slice: x: 2, y: 2, z: 4, core: 2. Of those that a mesh axis runs over, the one named last changes fastest.
Arguments:
- state: float32 [80, 131072], P('mem', 'grid'), may hold values from -6 to 6
- obs_tile: int32 [4], replicated, may hold values from 0 to 1023
- obs_offset: int32 [4, 256], replicated, may hold values from 0 to 127
- obs_value: float32 [4, 256], replicated, may hold values from -8 to 8
- obs_error: float32 [4, 256], replicated, may hold values from 0.5 to 4
- loc_mask: int32 [4, 1024], replicated, may hold values 0 or 1
- block_order: int32 [4], replicated, may hold values from 0 to 3, each once
Outputs:
- posterior: float32 [80, 131072], P('mem', 'grid')
The draws below stay inside these ranges and needn't reach their ends.
Inputs may be any that keep to these rules, and one draw needn't show every extreme that they name: `block_order`: a permutation of 0 to 3.
All inputs are finite; a program needn't handle non-finite values.
Results may differ from the reference program's by a relative error of at most 0.00024.
Values sent between devices are 32-bit elements; how exact they have to be, the bound alone decides.
No kernel may reach another device: no remote copies, remote signals or barrier semaphores. Data moves between devices by JAX's collectives and lax.ppermute only.
A program may use at most 64 MiB of HBM per device.

```python
import math
import jax
import jax.numpy as jnp
from jax import lax

MEMBERS = 80
OBS = 256
BLOCKS = 4
TILE = 128
VALUES = 131072
NTILES = 1024


def set_ends(values, stream_key, smallest, high):
    longest = values.shape.index(max(values.shape))
    spots = []
    for shift in (0, 1):
        where = [jax.random.randint(jax.random.fold_in(stream_key, axis), (), 0, length) for axis, length in enumerate(values.shape)]
        where[longest] = (where[longest] + shift) % values.shape[longest]
        spots.append(tuple(where))
    return values.at[spots[0]].set(smallest).at[spots[1]].set(high)


def block_levels(own_key, dims, shards, low, high):
    def one(axis_at, shards_of):
        steps = jax.random.uniform(jax.random.fold_in(jax.random.fold_in(own_key, 6), axis_at), (shards_of,), jnp.float32, low / len(shards), high / len(shards))
        return jnp.repeat(jnp.exp(steps), dims[axis_at] // shards_of).reshape((-1,) + (1,) * (len(dims) - axis_at - 1))

    gain = one(*shards[0])
    for cut in shards[1:]:
        gain = gain * one(*cut)
    return gain


def scatter_about(key, dims, deviation, reach, cuts=(), held_as=jnp.bfloat16):
    drawn = jax.random.normal(key, dims, jnp.float32) * deviation
    if len(cuts) > 0:
        drawn = block_levels(key, dims, cuts, -0.22, 0.18) * drawn
    return jnp.clip(drawn, min=-reach, max=reach).astype(held_as)


def setup_inputs(seed: int = 0) -> dict:
    key_of = jax.random.split(jax.random.key(seed), 8)
    return {
        "state": scatter_about(key_of[0], (MEMBERS, VALUES), 1.0, 6.0, ((0, 4), (1, 8)), jnp.float32),
        "obs_tile": set_ends(jax.random.randint(key_of[1], (BLOCKS,), 0, NTILES), jax.random.fold_in(key_of[1], 1), 0, NTILES - 1).astype(jnp.int32),
        "obs_offset": set_ends(jax.random.randint(key_of[2], (BLOCKS, OBS), 0, TILE), jax.random.fold_in(key_of[2], 1), 0, TILE - 1).astype(jnp.int32),
        "obs_value": scatter_about(key_of[3], (BLOCKS, OBS), 1.5, 8.0, (), jnp.float32),
        "obs_error": jnp.clip(jnp.exp(jax.random.uniform(key_of[4], (BLOCKS, OBS), jnp.float32, math.log(0.5), math.log(4.0))), 0.5, 4.0),
        "loc_mask": set_ends((jax.random.randint(key_of[5], (BLOCKS, NTILES), 0, 2) < 1).astype(jnp.int32), jax.random.fold_in(key_of[5], 1), 0, 1),
        "block_order": jax.random.permutation(key_of[6], BLOCKS).astype(jnp.int32),
    }


def reference(state, obs_tile, obs_offset, obs_value, obs_error, loc_mask, block_order):
    highest = lax.Precision.HIGHEST
    x_field = state
    for k in range(BLOCKS):
        b = block_order[k]
        start = (obs_tile[b] * TILE).astype(jnp.int32)
        slab = lax.dynamic_slice_in_dim(x_field, start, TILE, 1)
        prior = jnp.take(slab, obs_offset[b], axis=1)
        ybar = lax.optimization_barrier(jnp.mean(prior, axis=0))
        dev = prior - ybar
        var = lax.optimization_barrier(jnp.sum(dev * dev, axis=0)) / (MEMBERS - 1.0)
        error = obs_error[b]
        dy_inc = var / (var + error) * (obs_value[b] - ybar) + (jnp.sqrt(error / (var + error)) - 1.0) * dev
        weighted = dev / ((MEMBERS - 1.0) * (var + 1e-05))
        folded = jnp.dot(dy_inc, weighted.T, precision=highest)
        anom = x_field - lax.optimization_barrier(jnp.mean(x_field, axis=0))
        incr = jnp.dot(folded, anom, precision=highest)
        cols = jnp.repeat(loc_mask[b].astype(jnp.float32), TILE)
        x_field = x_field + incr * cols
    return x_field
```

```python
import functools
import math

import jax
import jax.numpy as jnp
from jax import lax
from jax.experimental import pallas as pl
from jax.experimental.pallas import tpu as pltpu
from jax.sharding import PartitionSpec as P

BLOCKS = 4
TILE = 128
HIGHEST = lax.Precision.HIGHEST
VMEM = pl.BlockSpec(memory_space=pltpu.VMEM)
SMEM = pl.BlockSpec(memory_space=pltpu.SMEM)


def pack_kernel(n_mem, parts, start_ref, x_ref, *outs):
    mem_loc = x_ref.shape[0]
    for d in range(n_mem):
        piece = outs[d]
        width = piece.shape[1]
        for p in range(parts):
            col = pl.multiple_of(start_ref[d] + p * width, TILE)
            piece[p * mem_loc : (p + 1) * mem_loc, :] = x_ref[:, pl.ds(col, width)]
    seen = outs[n_mem]
    for k in range(BLOCKS):
        col = pl.multiple_of(start_ref[n_mem + k], TILE)
        seen[k * mem_loc : (k + 1) * mem_loc, :] = x_ref[:, pl.ds(col, TILE)]


def pick_kernel(n_grid, shift_ref, *refs):
    out = refs[n_grid]
    mem_loc = out.shape[0] // BLOCKS
    for k in range(BLOCKS):
        rows = slice(k * mem_loc, (k + 1) * mem_loc)
        value = refs[0][rows, :]
        for d in range(1, n_grid):
            value = jnp.where(shift_ref[k] == d, refs[d][rows, :], value)
        out[rows, :] = value


def chain_kernel(n_mem, code_ref, offset_ref, value_ref, error_ref, *refs):
    pieces, out, slab = refs[:n_mem], refs[n_mem], refs[n_mem + 1]
    mem_loc = pieces[0].shape[0] // BLOCKS
    members = mem_loc * n_mem
    obs = offset_ref.shape[0]
    for d in range(n_mem):
        for k in range(BLOCKS):
            slab[k, d * mem_loc : (d + 1) * mem_loc, :] = pieces[d][k * mem_loc : (k + 1) * mem_loc, :]
    row = lax.broadcasted_iota(jnp.int32, (members, TILE), 0)
    lane = lax.broadcasted_iota(jnp.int32, (members, TILE), 1)
    out[:, 0:TILE] = jnp.where(row == lane, 1.0, 0.0)
    place = lax.broadcasted_iota(jnp.int32, (obs, TILE), 1)
    for k in range(BLOCKS):
        x = slab[k]
        ybar = jnp.sum(x, axis=0, keepdims=True) / members
        dev = x - ybar
        var = jnp.sum(dev * dev, axis=0, keepdims=True) / (members - 1.0)
        hit = offset_ref[:, k : k + 1] == place
        error = error_ref[:, k : k + 1]
        total = var + error
        shrink = jnp.where(hit, jnp.sqrt(error / total) - 1.0, 0.0)
        shift = jnp.where(hit, var / total * (value_ref[:, k : k + 1] - ybar), 0.0)
        scale = 1.0 / ((members - 1.0) * (var + 1e-05))
        shrink = jnp.sum(shrink, axis=0, keepdims=True) * scale
        shift = jnp.sum(shift, axis=0, keepdims=True) * scale
        centred = dev - jnp.sum(dev, axis=0, keepdims=True) / members
        gain = lax.dot_general(
            dev * shrink + shift,
            centred,
            (((1,), (1,)), ((), ())),
            precision=HIGHEST,
            preferred_element_type=jnp.float32,
        )
        for j in range(k + 1, BLOCKS):
            old = slab[j]
            new = old + jnp.dot(gain, old, precision=HIGHEST, preferred_element_type=jnp.float32)
            slab[j] = jnp.where(((code_ref[j] >> k) & 1) == 1, new, old)
        span = TILE << k
        so_far = out[:, 0:span]
        out[:, span : 2 * span] = so_far + jnp.dot(
            gain, so_far, precision=HIGHEST, preferred_element_type=jnp.float32
        )


def apply_kernel(n_mem, parts, code_ref, t_ref, *refs):
    pieces, outs = refs[:n_mem], refs[n_mem : 2 * n_mem]
    mem_loc = pieces[0].shape[0] // parts
    members = mem_loc * n_mem
    tiles = pieces[0].shape[1] // TILE
    for p in range(parts):
        rows = slice(p * mem_loc, (p + 1) * mem_loc)
        for t in range(tiles):
            cols = slice(t * TILE, (t + 1) * TILE)
            x = jnp.concatenate([piece[rows, cols] for piece in pieces], axis=0)
            first = pl.multiple_of(code_ref[p * tiles + t] * TILE, TILE)
            matrix = t_ref[:, pl.ds(first, TILE)][:, 0:members]
            y = jnp.dot(matrix, x, precision=HIGHEST, preferred_element_type=jnp.float32)
            for d in range(n_mem):
                outs[d][rows, cols] = y[d * mem_loc : (d + 1) * mem_loc, :]


def unpack_kernel(n_mem, parts, start_ref, *refs):
    out = refs[n_mem]
    mem_loc = out.shape[0]
    for d in range(n_mem):
        width = refs[d].shape[1]
        for p in range(parts):
            col = pl.multiple_of(start_ref[d] + p * width, TILE)
            out[:, pl.ds(col, width)] = refs[d][p * mem_loc : (p + 1) * mem_loc, :]


def on_device(state, obs_tile, obs_offset, obs_value, obs_error, loc_mask, block_order):
    f32 = jnp.float32
    n_mem = lax.axis_size("mem")
    n_grid = lax.axis_size("grid")
    mem_idx = lax.axis_index("mem")
    grid_idx = lax.axis_index("grid")
    mem_loc, grid_width = state.shape
    members = mem_loc * n_mem
    quarter = grid_width // n_mem
    parts = 8 // math.gcd(mem_loc, 8)
    piece = jax.ShapeDtypeStruct((parts * mem_loc, quarter // parts), f32)
    seen = jax.ShapeDtypeStruct((BLOCKS * mem_loc, TILE), f32)

    tile = obs_tile[block_order]
    tiles_here = grid_width // TILE
    masks = loc_mask[block_order]
    code = jnp.sum(masks << jnp.arange(BLOCKS, dtype=jnp.int32)[:, None], axis=0)
    code_here = lax.dynamic_slice_in_dim(
        code, grid_idx * tiles_here + mem_idx * (quarter // TILE), quarter // TILE
    )
    owner = tile // tiles_here
    starts = (mem_idx + jnp.arange(n_mem, dtype=jnp.int32)) % n_mem * quarter
    starts = jnp.concatenate([starts, tile % tiles_here * TILE])

    packed = pl.pallas_call(
        functools.partial(pack_kernel, n_mem, parts),
        out_shape=[piece] * n_mem + [seen],
        in_specs=[SMEM, VMEM],
        out_specs=[VMEM] * (n_mem + 1),
        name="pack",
    )(starts, state)
    own, mine = packed[0], packed[n_mem]

    def send(value, axis, size, by):
        return lax.ppermute(value, axis, [(j, (j + by) % size) for j in range(size)])

    candidates = [mine] + [send(mine, "grid", n_grid, d) for d in range(1, n_grid)]
    arrived = [own] + [send(packed[d], "mem", n_mem, d) for d in range(1, n_mem)]
    picked = pl.pallas_call(
        functools.partial(pick_kernel, n_grid),
        out_shape=seen,
        in_specs=[SMEM] + [VMEM] * n_grid,
        out_specs=VMEM,
        name="pick",
    )((grid_idx - owner) % n_grid, *candidates)
    slabs = [picked] + [send(picked, "mem", n_mem, d) for d in range(1, n_mem)]
    matrices = pl.pallas_call(
        functools.partial(chain_kernel, n_mem),
        out_shape=jax.ShapeDtypeStruct((members, TILE << BLOCKS), f32),
        in_specs=[SMEM] + [VMEM] * (3 + n_mem),
        out_specs=VMEM,
        scratch_shapes=[pltpu.VMEM((BLOCKS, members, TILE), f32)],
        name="chain",
    )(code[tile], obs_offset[block_order].T, obs_value[block_order].T, obs_error[block_order].T, *slabs)
    updated = pl.pallas_call(
        functools.partial(apply_kernel, n_mem, parts),
        out_shape=[piece] * n_mem,
        in_specs=[SMEM] + [VMEM] * (1 + n_mem),
        out_specs=[VMEM] * n_mem,
        name="apply",
    )(code_here, matrices, *arrived)
    back = [updated[0]] + [send(updated[d], "mem", n_mem, -d) for d in range(1, n_mem)]
    return pl.pallas_call(
        functools.partial(unpack_kernel, n_mem, parts),
        out_shape=jax.ShapeDtypeStruct(state.shape, f32),
        in_specs=[SMEM] + [VMEM] * n_mem,
        out_specs=VMEM,
        name="unpack",
    )(starts, *back)


def solution(mesh):
    placed = (P("mem", "grid"), P(), P(), P(), P(), P(), P())
    return jax.shard_map(
        on_device, mesh=mesh, in_specs=placed, out_specs=P("mem", "grid"), check_vma=False
    )
```

```python
import functools
import math

import jax
import jax.numpy as jnp
from jax import lax
from jax.experimental import pallas as pl
from jax.experimental.pallas import tpu as pltpu
from jax.sharding import PartitionSpec as P

BLOCKS = 4
TILE = 128
HIGHEST = lax.Precision.HIGHEST
VMEM = pl.BlockSpec(memory_space=pltpu.VMEM)
SMEM = pl.BlockSpec(memory_space=pltpu.SMEM)
ANY = pl.BlockSpec(memory_space=pl.ANY)


def piece_column(d, quarter, first):
    n_mem = lax.axis_size("mem")
    return lax.rem(lax.axis_index("mem") + d, n_mem) * quarter + first


def pack(x_ref, outs, parts, quarter, first):
    mem_loc = x_ref.shape[0]
    for d, out in enumerate(outs):
        width = out.shape[1]
        for p in range(parts):
            col = pl.multiple_of(piece_column(d, quarter, first) + p * width, TILE)
            out[p * mem_loc : (p + 1) * mem_loc, :] = x_ref[:, pl.ds(col, width)]


def first_kernel(parts, quarter, tile_ref, order_ref, x_ref, *outs):
    seen, outs = outs[-1], outs[:-1]
    mem_loc, grid_width = x_ref.shape
    for k in range(BLOCKS):
        tile = tile_ref[order_ref[k]]
        col = pl.multiple_of(lax.rem(tile, grid_width // TILE) * TILE, TILE)
        seen[k * mem_loc : (k + 1) * mem_loc, :] = x_ref[:, pl.ds(col, TILE)]
    pack(x_ref, outs, parts, quarter, 0)


def second_kernel(parts, quarter, first, order_ref, offset_ref, value_ref, error_ref, x_ref, after_ref, *outs):
    del after_ref
    pack(x_ref, outs[:-3], parts, quarter, first)
    obs = offset_ref.shape[1]
    for k in range(BLOCKS):
        row = pl.ds(order_ref[k], 1)
        for ref, out in zip((offset_ref, value_ref, error_ref), outs[-3:]):
            out[k] = jnp.transpose(jnp.broadcast_to(ref[row, :], (TILE, obs)))


def pick_kernel(tiles_here, tile_ref, order_ref, gathered_ref, out):
    mem_loc = out.shape[0] // BLOCKS
    for k in range(BLOCKS):
        owner = tile_ref[order_ref[k]] // tiles_here
        rows = slice(k * mem_loc, (k + 1) * mem_loc)
        out[rows, :] = gathered_ref[owner, rows, :]


def chain_kernel(n_mem, tile_ref, order_ref, mask_ref, offset_ref, value_ref, error_ref, *refs):
    pieces, out, slab = refs[:n_mem], refs[n_mem], refs[n_mem + 1]
    mem_loc = pieces[0].shape[0] // BLOCKS
    members = mem_loc * n_mem
    obs = offset_ref.shape[1]
    for d in range(n_mem):
        for k in range(BLOCKS):
            slab[k, d * mem_loc : (d + 1) * mem_loc, :] = pieces[d][k * mem_loc : (k + 1) * mem_loc, :]
    row = lax.broadcasted_iota(jnp.int32, (members, TILE), 0)
    lane = lax.broadcasted_iota(jnp.int32, (members, TILE), 1)
    out[:, 0:TILE] = jnp.where(row == lane, 1.0, 0.0)
    place = lax.broadcasted_iota(jnp.int32, (obs, TILE), 1)
    for k in range(BLOCKS):
        x = slab[k]
        ybar = jnp.sum(x, axis=0, keepdims=True) / members
        dev = x - ybar
        var = jnp.sum(dev * dev, axis=0, keepdims=True) / (members - 1.0)
        hit = offset_ref[k] == place
        error = error_ref[k]
        total = var + error
        shrink = jnp.where(hit, jnp.sqrt(error / total) - 1.0, 0.0)
        shift = jnp.where(hit, var / total * (value_ref[k] - ybar), 0.0)
        scale = 1.0 / ((members - 1.0) * (var + 1e-05))
        shrink = jnp.sum(shrink, axis=0, keepdims=True) * scale
        shift = jnp.sum(shift, axis=0, keepdims=True) * scale
        centred = dev - jnp.sum(dev, axis=0, keepdims=True) / members
        gain = lax.dot_general(
            dev * shrink + shift,
            centred,
            (((1,), (1,)), ((), ())),
            precision=HIGHEST,
            preferred_element_type=jnp.float32,
        )
        for j in range(k + 1, BLOCKS):
            old = slab[j]
            new = old + jnp.dot(gain, old, precision=HIGHEST, preferred_element_type=jnp.float32)
            used = mask_ref[order_ref[k], tile_ref[order_ref[j]]]
            slab[j] = jnp.where(used == 1, new, old)
        span = TILE << k
        so_far = out[:, 0:span]
        out[:, span : 2 * span] = so_far + jnp.dot(
            gain, so_far, precision=HIGHEST, preferred_element_type=jnp.float32
        )


def apply_kernel(n_mem, parts, quarter, first, order_ref, mask_ref, t_ref, *refs):
    pieces, outs = refs[:n_mem], refs[n_mem : 2 * n_mem]
    mem_loc = pieces[0].shape[0] // parts
    members = mem_loc * n_mem
    tiles = pieces[0].shape[1] // TILE
    base = (lax.axis_index("grid") * n_mem + lax.axis_index("mem")) * (quarter // TILE) + first // TILE
    for p in range(parts):
        rows = slice(p * mem_loc, (p + 1) * mem_loc)
        for t in range(tiles):
            cols = slice(t * TILE, (t + 1) * TILE)
            x = jnp.concatenate([piece[rows, cols] for piece in pieces], axis=0)
            code = 0
            for k in range(BLOCKS):
                code = code + (mask_ref[order_ref[k], base + p * tiles + t] << k)
            matrix = t_ref[:, pl.ds(pl.multiple_of(code * TILE, TILE), TILE)][:, 0:members]
            y = jnp.dot(matrix, x, precision=HIGHEST, preferred_element_type=jnp.float32)
            for d in range(n_mem):
                outs[d][rows, cols] = y[d * mem_loc : (d + 1) * mem_loc, :]


def unpack_kernel(n_mem, parts, quarter, firsts, *refs):
    out = refs[-1]
    mem_loc = out.shape[0]
    for c, first in enumerate(firsts):
        for d in range(n_mem):
            piece = refs[c * n_mem + d]
            width = piece.shape[1]
            for p in range(parts):
                col = pl.multiple_of(piece_column(d, quarter, first) + p * width, TILE)
                out[:, pl.ds(col, width)] = piece[p * mem_loc : (p + 1) * mem_loc, :]


def on_device(state, obs_tile, obs_offset, obs_value, obs_error, loc_mask, block_order):
    f32 = jnp.float32
    n_mem = lax.axis_size("mem")
    mem_loc, grid_width = state.shape
    members = mem_loc * n_mem
    quarter = grid_width // n_mem
    parts = 8 // math.gcd(mem_loc, 8)
    obs = obs_value.shape[1]
    unit = parts * TILE
    half = quarter // unit // 2 * unit
    firsts = (0, half)
    pieces = [
        jax.ShapeDtypeStruct((parts * mem_loc, width // parts), f32) for width in (half, quarter - half)
    ]
    seen = jax.ShapeDtypeStruct((BLOCKS * mem_loc, TILE), f32)
    dense = [jax.ShapeDtypeStruct((BLOCKS, obs, TILE), kind) for kind in (jnp.int32, f32, f32)]

    def send(value, by):
        return lax.ppermute(value, "mem", [(j, (j + by) % n_mem) for j in range(n_mem)])

    def exchange(values, sign):
        return [values[0]] + [send(values[d], sign * d) for d in range(1, n_mem)]

    *chunk, mine = pl.pallas_call(
        functools.partial(first_kernel, parts, quarter),
        out_shape=[pieces[0]] * n_mem + [seen],
        in_specs=[SMEM, SMEM, VMEM],
        out_specs=[VMEM] * (n_mem + 1),
        name="first",
    )(obs_tile, block_order, state)
    gathered = lax.all_gather(mine, "grid", axis=0)
    arrived_a = exchange(chunk, 1)
    picked = pl.pallas_call(
        functools.partial(pick_kernel, grid_width // TILE),
        out_shape=seen,
        in_specs=[SMEM, SMEM, VMEM],
        out_specs=VMEM,
        name="pick",
    )(obs_tile, block_order, gathered)
    slabs = exchange([picked] * n_mem, 1)
    *chunk, offset, value, error = pl.pallas_call(
        functools.partial(second_kernel, parts, quarter, half),
        out_shape=[pieces[1]] * n_mem + dense,
        in_specs=[SMEM] + [VMEM] * 4 + [ANY],
        out_specs=[VMEM] * (n_mem + 3),
        name="second",
    )(block_order, obs_offset, obs_value, obs_error, state, picked)
    arrived_b = exchange(chunk, 1)
    matrices = pl.pallas_call(
        functools.partial(chain_kernel, n_mem),
        out_shape=jax.ShapeDtypeStruct((members, TILE << BLOCKS), f32),
        in_specs=[SMEM] * 3 + [VMEM] * (3 + n_mem),
        out_specs=VMEM,
        scratch_shapes=[pltpu.VMEM((BLOCKS, members, TILE), f32)],
        name="chain",
    )(obs_tile, block_order, loc_mask, offset, value, error, *slabs)
    back = []
    for arrived, piece, first in zip((arrived_a, arrived_b), pieces, firsts):
        updated = pl.pallas_call(
            functools.partial(apply_kernel, n_mem, parts, quarter, first),
            out_shape=[piece] * n_mem,
            in_specs=[SMEM] * 2 + [VMEM] * (1 + n_mem),
            out_specs=[VMEM] * n_mem,
            name="apply",
        )(block_order, loc_mask, matrices, *arrived)
        back += exchange(updated, -1)
    return pl.pallas_call(
        functools.partial(unpack_kernel, n_mem, parts, quarter, firsts),
        out_shape=jax.ShapeDtypeStruct(state.shape, f32),
        in_specs=[VMEM] * len(back),
        out_specs=VMEM,
        name="unpack",
    )(*back)


def solution(mesh):
    placed = (P("mem", "grid"), P(), P(), P(), P(), P(), P())
    return jax.shard_map(
        on_device, mesh=mesh, in_specs=placed, out_specs=P("mem", "grid"), check_vma=False
    )
```

```python
import functools
import math

import jax
import jax.numpy as jnp
from jax import lax
from jax.experimental import pallas as pl
from jax.experimental.pallas import tpu as pltpu
from jax.sharding import PartitionSpec as P

BLOCKS = 4
TILE = 128
HIGHEST = lax.Precision.HIGHEST
VMEM = pl.BlockSpec(memory_space=pltpu.VMEM)
SMEM = pl.BlockSpec(memory_space=pltpu.SMEM)
ANY = pl.BlockSpec(memory_space=pl.ANY)
HBM = pl.BlockSpec(memory_space=pltpu.HBM)


def kernel_call(kernel, name, out_shape, in_specs, out_specs, scratch_shapes=(), aliases=None, vmem=12):
    return pl.pallas_call(
        kernel,
        name=name,
        out_shape=out_shape,
        in_specs=in_specs,
        out_specs=out_specs,
        scratch_shapes=scratch_shapes,
        input_output_aliases=aliases or {},
        compiler_params=pltpu.CompilerParams(vmem_limit_bytes=vmem << 20),
    )


def run_all(copies):
    for copy in copies:
        copy.start()
    for copy in copies:
        copy.wait()


def seen_kernel(tile_ref, order_ref, x_ref, out, tile, order, held, sem):
    mem_loc, grid_width = x_ref.shape
    tiles_here = grid_width // TILE
    run_all(
        [
            pltpu.make_async_copy(tile_ref, tile, sem.at[0]),
            pltpu.make_async_copy(order_ref, order, sem.at[1]),
        ]
    )
    copies = []
    for k in range(BLOCKS):
        col = pl.multiple_of(lax.rem(tile[order[k]], tiles_here) * TILE, TILE)
        copies.append(pltpu.make_async_copy(x_ref.at[:, pl.ds(col, TILE)], held.at[k], sem.at[k]))
    run_all(copies)
    for k in range(BLOCKS):
        here = tile[order[k]] // tiles_here == lax.axis_index("grid")
        out[k * mem_loc : (k + 1) * mem_loc, :] = jnp.where(here, held[k], 0.0)


def piece_columns(d, quarter, first, width):
    return pl.ds(pl.multiple_of((lax.axis_index("mem") ^ d) * quarter + first, TILE), width)


def pack_kernel(parts, quarter, jobs, x_ref, after_ref, *outs):
    del after_ref
    mem_loc = x_ref.shape[0]
    for (d, chunks), out in zip(jobs, outs):
        to = 0
        for first, width in chunks:
            width = width // parts
            for p in range(parts):
                cols = piece_columns(d, quarter, first + p * width, width)
                out[p * mem_loc : (p + 1) * mem_loc, to : to + width] = x_ref[:, cols]
            to += width


def unpack_kernel(parts, quarter, first, pieces, *refs):
    out, held, sem = refs[-3:]
    mem_loc = out.shape[0]
    copies = []
    for i, d in enumerate(pieces):
        width = refs[i].shape[1]
        for p in range(parts):
            held[i, :, p * width : (p + 1) * width] = refs[i][p * mem_loc : (p + 1) * mem_loc, :]
        cols = piece_columns(d, quarter, first, parts * width)
        copies.append(pltpu.make_async_copy(held.at[i], out.at[:, cols], sem.at[i]))
        copies[i].start()
    for copy in copies:
        copy.wait()


def chain_kernel(
    places, tile_ref, order_ref, mask_ref, offset_ref, value_ref, error_ref, one_ref, two_ref, out, slab, rows_ref
):
    members = slab.shape[1]
    mem_loc = members // len(places)
    obs = offset_ref.shape[1]
    for k in range(BLOCKS):
        for i, ref in enumerate((offset_ref, value_ref, error_ref)):
            rows_ref[3 * k + i : 3 * k + i + 1, :] = ref[pl.ds(order_ref[k], 1), :].astype(jnp.float32)
    columns = jnp.transpose(rows_ref[...])
    for i, d in enumerate(places):
        for k in range(BLOCKS):
            rows = slice((i * BLOCKS + k) * mem_loc, (i * BLOCKS + k + 1) * mem_loc)
            slab[k, d * mem_loc : (d + 1) * mem_loc, :] = one_ref[rows, :] + two_ref[rows, :]
    row = lax.broadcasted_iota(jnp.int32, (members, TILE), 0)
    lane = lax.broadcasted_iota(jnp.int32, (members, TILE), 1)
    out[:, 0:TILE] = jnp.where(row == lane, 1.0, 0.0)
    place = lax.broadcasted_iota(jnp.int32, (obs, TILE), 1).astype(jnp.float32)
    for k in range(BLOCKS):
        x = slab[k]
        ybar = jnp.sum(x, axis=0, keepdims=True) / members
        dev = x - ybar
        var = jnp.sum(dev * dev, axis=0, keepdims=True) / (members - 1.0)
        offset, value, error = (columns[:, 3 * k + i : 3 * k + i + 1] for i in range(3))
        hit = offset == place
        total = var + error
        shrink = jnp.where(hit, jnp.sqrt(error / total) - 1.0, 0.0)
        shift = jnp.where(hit, var / total * (value - ybar), 0.0)
        scale = 1.0 / ((members - 1.0) * (var + 1e-05))
        shrink = jnp.sum(shrink, axis=0, keepdims=True) * scale
        shift = jnp.sum(shift, axis=0, keepdims=True) * scale
        centred = dev - jnp.sum(dev, axis=0, keepdims=True) / members
        gain = lax.dot_general(
            dev * shrink + shift,
            centred,
            (((1,), (1,)), ((), ())),
            precision=HIGHEST,
            preferred_element_type=jnp.float32,
        )
        for j in range(k + 1, BLOCKS):
            old = slab[j]
            new = old + jnp.dot(gain, old, precision=HIGHEST, preferred_element_type=jnp.float32)
            used = mask_ref[order_ref[k], tile_ref[order_ref[j]]]
            slab[j] = jnp.where(used == 1, new, old)
        span = TILE << k
        so_far = out[:, 0:span]
        out[:, span : 2 * span] = so_far + jnp.dot(
            gain, so_far, precision=HIGHEST, preferred_element_type=jnp.float32
        )


def apply_kernel(n_mem, parts, quarter, first, starts, order_ref, mask_ref, t_ref, *refs):
    pieces, outs = refs[:n_mem], refs[n_mem : 2 * n_mem]
    mem_loc = pieces[0].shape[0] // parts
    members = mem_loc * n_mem
    tiles = outs[0].shape[1] // TILE
    base = (lax.axis_index("grid") * n_mem + lax.axis_index("mem")) * (quarter // TILE) + first // TILE
    for p in range(parts):
        rows = slice(p * mem_loc, (p + 1) * mem_loc)
        for t in range(tiles):
            cols = slice(t * TILE, (t + 1) * TILE)
            x = jnp.concatenate(
                [piece[rows, start + t * TILE : start + (t + 1) * TILE] for piece, start in zip(pieces, starts)],
                axis=0,
            )
            code = 0
            for k in range(BLOCKS):
                code = code + (mask_ref[order_ref[k], base + p * tiles + t] << k)
            matrix = t_ref[:, pl.ds(pl.multiple_of(code * TILE, TILE), TILE)][:, 0:members]
            y = jnp.dot(matrix, x, precision=HIGHEST, preferred_element_type=jnp.float32)
            for d in range(n_mem):
                outs[d][rows, cols] = y[d * mem_loc : (d + 1) * mem_loc, :]


def on_device(state, obs_tile, obs_offset, obs_value, obs_error, loc_mask, block_order):
    f32 = jnp.float32
    n_mem = lax.axis_size("mem")
    n_grid = lax.axis_size("grid")
    mem_loc, grid_width = state.shape
    members = mem_loc * n_mem
    quarter = grid_width // n_mem
    parts = 8 // math.gcd(mem_loc, 8)
    obs = obs_value.shape[1]
    unit = parts * TILE
    half = quarter // unit * 8 // 16 * unit
    firsts = (0, half)
    widths = (half, quarter - half)
    pieces = [jax.ShapeDtypeStruct((parts * mem_loc, width // parts), f32) for width in widths]

    def swap(value, axis, by):
        return lax.ppermute(value, axis, [(j, j ^ by) for j in range(lax.axis_size(axis))])

    def pack(jobs, after):
        chunks = [(d, [(firsts[c], widths[c]) for c in which]) for d, which in jobs]
        total = [sum(width for _, width in each) for _, each in chunks]
        return kernel_call(
            functools.partial(pack_kernel, parts, quarter, chunks),
            "pack",
            [jax.ShapeDtypeStruct((parts * mem_loc, width // parts), f32) for width in total],
            [VMEM, ANY],
            [VMEM] * len(jobs),
        )(state, after)

    def update_matrices(slab):
        hop = 1
        while True:
            other = swap(slab, "grid", hop)
            hop *= 2
            if hop >= n_grid:
                break
            slab = slab + other
        return kernel_call(
            functools.partial(chain_kernel, places),
            "chain",
            jax.ShapeDtypeStruct((members, TILE << BLOCKS), f32),
            [SMEM] * 3 + [VMEM] * 5,
            VMEM,
            [pltpu.VMEM((BLOCKS, members, TILE), f32), pltpu.VMEM((TILE, obs), f32)],
        )(obs_tile, block_order, loc_mask, obs_offset, obs_value, obs_error, slab, other)

    def no_updates(slab):
        return jnp.tile(jnp.eye(members, TILE, dtype=f32), (1, 1 << BLOCKS))

    mine = kernel_call(
        seen_kernel,
        "seen",
        jax.ShapeDtypeStruct((BLOCKS * mem_loc, TILE), f32),
        [HBM] * 3,
        VMEM,
        [
            pltpu.SMEM((BLOCKS,), jnp.int32),
            pltpu.SMEM((BLOCKS,), jnp.int32),
            pltpu.VMEM((BLOCKS, mem_loc, TILE), f32),
            pltpu.SemaphoreType.DMA((BLOCKS,)),
        ],
        vmem=12,
    )(obs_tile, block_order, state)
    places = range(n_mem)
    seen = [mine] + [swap(mine, "mem", d) for d in places[1:]]
    slab = jnp.concatenate(seen, axis=0)
    held = {}

    def start(jobs, after):
        for job, value in zip(jobs, pack(jobs, after)):
            held[job] = swap(value, "mem", job[0]) if job[0] else value

    start([(d, (0, 1)) for d in range(n_mem - 1)] + [(n_mem - 1, (0,))], slab)
    matrices = lax.cond(jnp.any(loc_mask > 0), update_matrices, no_updates, slab)
    start([(n_mem - 1, (1,))], matrices)
    arrived, starts = [], []
    for c in range(2):
        arrived.append([held.get((d, (c,)), held.get((d, (0, 1)))) for d in range(n_mem)])
        starts.append([0 if (d, (c,)) in held else firsts[c] // parts for d in range(n_mem)])
    result = []
    for c in range(2):
        updated = kernel_call(
            functools.partial(apply_kernel, n_mem, parts, quarter, firsts[c], starts[c]),
            "apply",
            [pieces[c]] * n_mem,
            [SMEM] * 2 + [VMEM] * (1 + n_mem),
            [VMEM] * n_mem,
        )(block_order, loc_mask, matrices, *arrived[c])
        back = [updated[0]] + [swap(updated[d], "mem", d) for d in range(1, n_mem)]
        result = kernel_call(
            functools.partial(unpack_kernel, parts, quarter, firsts[c], range(n_mem)),
            "unpack",
            [jax.ShapeDtypeStruct(state.shape, f32)],
            [VMEM] * n_mem + [HBM] * len(result),
            [HBM],
            [pltpu.VMEM((n_mem, mem_loc, widths[c]), f32), pltpu.SemaphoreType.DMA((n_mem,))],
            {n_mem: 0} if result else None,
        )(*back, *result)
    return result[0]


def solution(mesh):
    placed = (P("mem", "grid"), P(), P(), P(), P(), P(), P())
    return jax.shard_map(
        on_device, mesh=mesh, in_specs=placed, out_specs=P("mem", "grid"), check_vma=False
    )
```

```python
import functools
import math

import jax
import jax.numpy as jnp
from jax import lax
from jax.experimental import pallas as pl
from jax.experimental.pallas import tpu as pltpu
from jax.sharding import PartitionSpec as P

BLOCKS = 4
TILE = 128
HIGHEST = lax.Precision.HIGHEST
VMEM = pl.BlockSpec(memory_space=pltpu.VMEM)
SMEM = pl.BlockSpec(memory_space=pltpu.SMEM)
ANY = pl.BlockSpec(memory_space=pl.ANY)
HBM = pl.BlockSpec(memory_space=pltpu.HBM)


def kernel_call(kernel, name, out_shape, in_specs, out_specs, scratch_shapes=(), aliases=None, vmem=12):
    return pl.pallas_call(
        kernel,
        name=name,
        out_shape=out_shape,
        in_specs=in_specs,
        out_specs=out_specs,
        scratch_shapes=scratch_shapes,
        input_output_aliases=aliases or {},
        compiler_params=pltpu.CompilerParams(vmem_limit_bytes=vmem << 20),
    )


def run_all(copies):
    for copy in copies:
        copy.start()
    for copy in copies:
        copy.wait()


def seen_kernel(tile_ref, order_ref, x_ref, out, tile, order, sem):
    mem_loc, grid_width = x_ref.shape
    tiles_here = grid_width // TILE
    run_all(
        [
            pltpu.make_async_copy(tile_ref, tile, sem.at[0]),
            pltpu.make_async_copy(order_ref, order, sem.at[1]),
        ]
    )
    for k in range(BLOCKS):
        at = tile[order[k]]
        cols = pl.ds(pl.multiple_of(lax.rem(at, tiles_here) * TILE, TILE), TILE)
        here = at // tiles_here == lax.axis_index("grid")
        out[k * mem_loc : (k + 1) * mem_loc, :] = jnp.where(here, x_ref[:, cols], 0.0)


def piece_columns(d, quarter, first, width):
    return pl.ds(pl.multiple_of((lax.axis_index("mem") ^ d) * quarter + first, TILE), width)


def pack_kernel(parts, quarter, jobs, x_ref, *refs):
    outs = refs[-len(jobs) :]
    mem_loc = x_ref.shape[0]
    for (d, chunks), out in zip(jobs, outs):
        to = 0
        for first, width in chunks:
            width = width // parts
            for p in range(parts):
                cols = piece_columns(d, quarter, first + p * width, width)
                out[p * mem_loc : (p + 1) * mem_loc, to : to + width] = x_ref[:, cols]
            to += width


def unpack_kernel(parts, quarter, chunks, n_mem, *refs):
    out, held, sem = refs[-3:]
    mem_loc = out.shape[0]
    copies = []
    for d in range(n_mem):
        at = 0
        for first, width in chunks:
            side = width // parts
            for p in range(parts):
                part = refs[d][p * mem_loc : (p + 1) * mem_loc, at // parts : at // parts + side]
                held[d, :, at + p * side : at + (p + 1) * side] = part
            at += width
        first, total = chunks[0][0], sum(width for _, width in chunks)
        copies.append(
            pltpu.make_async_copy(held.at[d], out.at[:, piece_columns(d, quarter, first, total)], sem.at[d])
        )
        copies[d].start()
    for copy in copies:
        copy.wait()


def join_kernel(count, *refs):
    rows = refs[0].shape[0]
    for i in range(count):
        refs[-1][i * rows : (i + 1) * rows, :] = refs[i][...]


def chain_kernel(
    places, tile_ref, order_ref, mask_ref, offset_ref, value_ref, error_ref, one_ref, two_ref, out, slab, rows_ref
):
    members = slab.shape[1]
    mem_loc = members // len(places)
    obs = offset_ref.shape[1]
    for k in range(BLOCKS):
        for i, ref in enumerate((offset_ref, value_ref, error_ref)):
            rows_ref[3 * k + i : 3 * k + i + 1, :] = ref[pl.ds(order_ref[k], 1), :].astype(jnp.float32)
    columns = jnp.transpose(rows_ref[...])
    for i, d in enumerate(places):
        for k in range(BLOCKS):
            rows = slice((i * BLOCKS + k) * mem_loc, (i * BLOCKS + k + 1) * mem_loc)
            slab[k, d * mem_loc : (d + 1) * mem_loc, :] = one_ref[rows, :] + two_ref[rows, :]
    row = lax.broadcasted_iota(jnp.int32, (members, TILE), 0)
    lane = lax.broadcasted_iota(jnp.int32, (members, TILE), 1)
    out[:, 0:TILE] = jnp.where(row == lane, 1.0, 0.0)
    place = lax.broadcasted_iota(jnp.int32, (obs, TILE), 1).astype(jnp.float32)
    for k in range(BLOCKS):
        x = slab[k]
        ybar = jnp.sum(x, axis=0, keepdims=True) / members
        dev = x - ybar
        var = jnp.sum(dev * dev, axis=0, keepdims=True) / (members - 1.0)
        offset, value, error = (columns[:, 3 * k + i : 3 * k + i + 1] for i in range(3))
        hit = offset == place
        total = var + error
        shrink = jnp.where(hit, jnp.sqrt(error / total) - 1.0, 0.0)
        shift = jnp.where(hit, var / total * (value - ybar), 0.0)
        scale = 1.0 / ((members - 1.0) * (var + 1e-05))
        shrink = jnp.sum(shrink, axis=0, keepdims=True) * scale
        shift = jnp.sum(shift, axis=0, keepdims=True) * scale
        centred = dev - jnp.sum(dev, axis=0, keepdims=True) / members
        gain = lax.dot_general(
            dev * shrink + shift,
            centred,
            (((1,), (1,)), ((), ())),
            precision=HIGHEST,
            preferred_element_type=jnp.float32,
        )
        for j in range(k + 1, BLOCKS):
            old = slab[j]
            new = old + jnp.dot(gain, old, precision=HIGHEST, preferred_element_type=jnp.float32)
            used = mask_ref[order_ref[k], tile_ref[order_ref[j]]]
            slab[j] = jnp.where(used == 1, new, old)
        span = TILE << k
        so_far = out[:, 0:span]
        out[:, span : 2 * span] = so_far + jnp.dot(
            gain, so_far, precision=HIGHEST, preferred_element_type=jnp.float32
        )


def apply_kernel(n_mem, parts, quarter, chunks, order_ref, mask_ref, t_ref, *refs):
    refs, outs = refs[:-n_mem], refs[-n_mem:]
    mem_loc = outs[0].shape[0] // parts
    members = mem_loc * n_mem
    base = (lax.axis_index("grid") * n_mem + lax.axis_index("mem")) * (quarter // TILE)
    at = 0
    for first, width, sources in chunks:
        tiles = width // parts // TILE
        for p in range(parts):
            rows = slice(p * mem_loc, (p + 1) * mem_loc)
            for t in range(tiles):
                x = jnp.concatenate(
                    [refs[i][rows, start + t * TILE : start + (t + 1) * TILE] for i, start in sources], axis=0
                )
                code = 0
                for k in range(BLOCKS):
                    code = code + (mask_ref[order_ref[k], base + first // TILE + p * tiles + t] << k)
                matrix = t_ref[:, pl.ds(pl.multiple_of(code * TILE, TILE), TILE)][:, 0:members]
                y = jnp.dot(matrix, x, precision=HIGHEST, preferred_element_type=jnp.float32)
                for d in range(n_mem):
                    outs[d][rows, at + t * TILE : at + (t + 1) * TILE] = y[d * mem_loc : (d + 1) * mem_loc, :]
        at += width // parts


def on_device(state, obs_tile, obs_offset, obs_value, obs_error, loc_mask, block_order):
    f32 = jnp.float32
    n_mem = lax.axis_size("mem")
    n_grid = lax.axis_size("grid")
    mem_loc, grid_width = state.shape
    members = mem_loc * n_mem
    quarter = grid_width // n_mem
    parts = 8 // math.gcd(mem_loc, 8)
    obs = obs_value.shape[1]
    unit = parts * TILE
    units = quarter // unit
    cuts = [units * cut // 16 * unit for cut in (8,)]
    firsts = [0] + cuts
    widths = [end - first for first, end in zip(firsts, cuts + [quarter])]
    every = tuple(range(len(firsts)))

    def swap(value, axis, by):
        return lax.ppermute(value, axis, [(j, j ^ by) for j in range(lax.axis_size(axis))])

    def pack(jobs, *after):
        chunks = [(d, [(firsts[c], widths[c]) for c in which]) for d, which in jobs]
        total = [sum(width for _, width in each) for _, each in chunks]
        return kernel_call(
            functools.partial(pack_kernel, parts, quarter, chunks),
            "pack",
            [jax.ShapeDtypeStruct((parts * mem_loc, width // parts), f32) for width in total],
            [VMEM] + [ANY] * len(after),
            [VMEM] * len(jobs),
        )(state, *after)

    def update_matrices(slab):
        hop = 1
        while True:
            other = swap(slab, "grid", hop)
            hop *= 2
            if hop >= n_grid:
                break
            slab = slab + other
        return kernel_call(
            functools.partial(chain_kernel, places),
            "chain",
            jax.ShapeDtypeStruct((members, TILE << BLOCKS), f32),
            [SMEM] * 3 + [VMEM] * 5,
            VMEM,
            [pltpu.VMEM((BLOCKS, members, TILE), f32), pltpu.VMEM((TILE, obs), f32)],
        )(obs_tile, block_order, loc_mask, obs_offset, obs_value, obs_error, slab, other)

    def no_updates(slab):
        return jnp.tile(jnp.eye(members, TILE, dtype=f32), (1, 1 << BLOCKS))

    mine = kernel_call(
        seen_kernel,
        "seen",
        jax.ShapeDtypeStruct((BLOCKS * mem_loc, TILE), f32),
        [HBM, HBM, VMEM],
        VMEM,
        [
            pltpu.SMEM((BLOCKS,), jnp.int32),
            pltpu.SMEM((BLOCKS,), jnp.int32),
            pltpu.SemaphoreType.DMA((2,)),
        ],
    )(obs_tile, block_order, state)
    places = range(n_mem)
    seen = [mine] + [swap(mine, "mem", d) for d in places[1:]]
    held = {}

    def start(jobs, *after):
        for job, value in zip(jobs, pack(jobs, *after)):
            held[job] = swap(value, "mem", job[0]) if job[0] else value

    last = n_mem - 1

    start([(d, every) for d in range(last)] + [(last, (0,)), (last, (1,))], *seen)

    slab = kernel_call(
        functools.partial(join_kernel, n_mem),
        "join",
        jax.ShapeDtypeStruct((n_mem * BLOCKS * mem_loc, TILE), f32),
        [VMEM] * n_mem,
        VMEM,
    )(*seen)
    matrices = lax.cond(jnp.any(loc_mask > 0), update_matrices, no_updates, slab)
    result = []
    for group in ((0,), (1,)):
        jobs = sorted({job for job in held if set(job[1]) & set(group)})
        chunks = []
        for c in group:
            sources = []
            for d in range(n_mem):
                job = next(job for job in jobs if job[0] == d and c in job[1])
                sources.append((jobs.index(job), sum(widths[b] for b in job[1] if b < c) // parts))
            chunks.append((firsts[c], widths[c], sources))
        total = sum(widths[c] for c in group)
        updated = kernel_call(
            functools.partial(apply_kernel, n_mem, parts, quarter, chunks),
            "apply",
            [jax.ShapeDtypeStruct((parts * mem_loc, total // parts), f32)] * n_mem,
            [SMEM] * 2 + [VMEM] * (1 + len(jobs)),
            [VMEM] * n_mem,
        )(block_order, loc_mask, matrices, *[held[job] for job in jobs])
        back = [updated[0]] + [swap(updated[d], "mem", d) for d in range(1, n_mem)]
        result = kernel_call(
            functools.partial(unpack_kernel, parts, quarter, [chunk[:2] for chunk in chunks], n_mem),
            "unpack",
            [jax.ShapeDtypeStruct(state.shape, f32)],
            [VMEM] * n_mem + [HBM] * len(result),
            [HBM],
            [pltpu.VMEM((n_mem, mem_loc, total), f32), pltpu.SemaphoreType.DMA((n_mem,))],
            {n_mem: 0} if result else None,
        )(*back, *result)
    return result[0]


def solution(mesh):
    placed = (P("mem", "grid"), P(), P(), P(), P(), P(), P())
    return jax.shard_map(
        on_device, mesh=mesh, in_specs=placed, out_specs=P("mem", "grid"), check_vma=False
    )
```

```python
import functools
import math

import jax
import jax.numpy as jnp
from jax import lax
from jax.experimental import pallas as pl
from jax.experimental.pallas import tpu as pltpu
from jax.sharding import PartitionSpec as P

BLOCKS = 4
TILE = 128
HIGHEST = lax.Precision.HIGHEST
VMEM = pl.BlockSpec(memory_space=pltpu.VMEM)
SMEM = pl.BlockSpec(memory_space=pltpu.SMEM)
ANY = pl.BlockSpec(memory_space=pl.ANY)
HBM = pl.BlockSpec(memory_space=pltpu.HBM)


def kernel_call(kernel, name, out_shape, in_specs, out_specs, scratch_shapes=(), aliases=None, vmem=12):
    return pl.pallas_call(
        kernel,
        name=name,
        out_shape=out_shape,
        in_specs=in_specs,
        out_specs=out_specs,
        scratch_shapes=scratch_shapes,
        input_output_aliases=aliases or {},
        compiler_params=pltpu.CompilerParams(vmem_limit_bytes=vmem << 20),
    )


def run_all(copies):
    for copy in copies:
        copy.start()
    for copy in copies:
        copy.wait()


def seen_kernel(tile_ref, order_ref, x_ref, out, tile, order, sem):
    mem_loc, grid_width = x_ref.shape
    tiles_here = grid_width // TILE
    run_all(
        [
            pltpu.make_async_copy(tile_ref, tile, sem.at[0]),
            pltpu.make_async_copy(order_ref, order, sem.at[1]),
        ]
    )
    for k in range(BLOCKS):
        at = tile[order[k]]
        cols = pl.ds(pl.multiple_of(lax.rem(at, tiles_here) * TILE, TILE), TILE)
        here = at // tiles_here == lax.axis_index("grid")
        out[k * mem_loc : (k + 1) * mem_loc, :] = jnp.where(here, x_ref[:, cols], 0.0)


def piece_columns(d, quarter, first, width):
    return pl.ds(pl.multiple_of((lax.axis_index("mem") ^ d) * quarter + first, TILE), width)


def pack_kernel(parts, quarter, jobs, x_ref, *refs):
    outs = refs[-len(jobs) :]
    mem_loc = x_ref.shape[0]
    for (d, chunks), out in zip(jobs, outs):
        to = 0
        for first, width in chunks:
            width = width // parts
            for p in range(parts):
                cols = piece_columns(d, quarter, first + p * width, width)
                out[p * mem_loc : (p + 1) * mem_loc, to : to + width] = x_ref[:, cols]
            to += width


def unpack_kernel(parts, quarter, chunks, shifts, *refs):
    out, held, sem = refs[-3:]
    mem_loc = out.shape[0]
    copies = []
    for i, d in enumerate(shifts):
        at = 0
        for first, width in chunks:
            side = width // parts
            for p in range(parts):
                part = refs[i][p * mem_loc : (p + 1) * mem_loc, at // parts : at // parts + side]
                held[i, :, at + p * side : at + (p + 1) * side] = part
            at += width
        first, total = chunks[0][0], sum(width for _, width in chunks)
        copies.append(
            pltpu.make_async_copy(held.at[i], out.at[:, piece_columns(d, quarter, first, total)], sem.at[i])
        )
        copies[i].start()
    for copy in copies:
        copy.wait()


def join_kernel(count, *refs):
    rows = refs[0].shape[0]
    for i in range(count):
        refs[-1][i * rows : (i + 1) * rows, :] = refs[i][...]


def chain_kernel(
    places, tile_ref, order_ref, mask_ref, offset_ref, value_ref, error_ref, one_ref, two_ref, out, slab, rows_ref
):
    members = slab.shape[1]
    mem_loc = members // len(places)
    obs = offset_ref.shape[1]
    for k in range(BLOCKS):
        for i, ref in enumerate((offset_ref, value_ref, error_ref)):
            rows_ref[3 * k + i : 3 * k + i + 1, :] = ref[pl.ds(order_ref[k], 1), :].astype(jnp.float32)
    columns = jnp.transpose(rows_ref[...])
    for i, d in enumerate(places):
        for k in range(BLOCKS):
            rows = slice((i * BLOCKS + k) * mem_loc, (i * BLOCKS + k + 1) * mem_loc)
            slab[k, d * mem_loc : (d + 1) * mem_loc, :] = one_ref[rows, :] + two_ref[rows, :]
    row = lax.broadcasted_iota(jnp.int32, (members, TILE), 0)
    lane = lax.broadcasted_iota(jnp.int32, (members, TILE), 1)
    out[:, 0:TILE] = jnp.where(row == lane, 1.0, 0.0)
    place = lax.broadcasted_iota(jnp.int32, (obs, TILE), 1).astype(jnp.float32)
    for k in range(BLOCKS):
        x = slab[k]
        ybar = jnp.sum(x, axis=0, keepdims=True) / members
        dev = x - ybar
        var = jnp.sum(dev * dev, axis=0, keepdims=True) / (members - 1.0)
        offset, value, error = (columns[:, 3 * k + i : 3 * k + i + 1] for i in range(3))
        hit = offset == place
        total = var + error
        shrink = jnp.where(hit, jnp.sqrt(error / total) - 1.0, 0.0)
        shift = jnp.where(hit, var / total * (value - ybar), 0.0)
        scale = 1.0 / ((members - 1.0) * (var + 1e-05))
        shrink = jnp.sum(shrink, axis=0, keepdims=True) * scale
        shift = jnp.sum(shift, axis=0, keepdims=True) * scale
        centred = dev - jnp.sum(dev, axis=0, keepdims=True) / members
        gain = lax.dot_general(
            dev * shrink + shift,
            centred,
            (((1,), (1,)), ((), ())),
            precision=HIGHEST,
            preferred_element_type=jnp.float32,
        )
        for j in range(k + 1, BLOCKS):
            old = slab[j]
            new = old + jnp.dot(gain, old, precision=HIGHEST, preferred_element_type=jnp.float32)
            used = mask_ref[order_ref[k], tile_ref[order_ref[j]]]
            slab[j] = jnp.where(used == 1, new, old)
        span = TILE << k
        so_far = out[:, 0:span]
        out[:, span : 2 * span] = so_far + jnp.dot(
            gain, so_far, precision=HIGHEST, preferred_element_type=jnp.float32
        )


def apply_kernel(n_mem, parts, quarter, chunks, order_ref, mask_ref, t_ref, *refs):
    refs, outs = refs[:-n_mem], refs[-n_mem:]
    mem_loc = outs[0].shape[0] // parts
    members = mem_loc * n_mem
    base = (lax.axis_index("grid") * n_mem + lax.axis_index("mem")) * (quarter // TILE)
    at = 0
    for first, width, sources in chunks:
        tiles = width // parts // TILE
        for p in range(parts):
            rows = slice(p * mem_loc, (p + 1) * mem_loc)
            for t in range(tiles):
                x = jnp.concatenate(
                    [refs[i][rows, start + t * TILE : start + (t + 1) * TILE] for i, start in sources], axis=0
                )
                code = 0
                for k in range(BLOCKS):
                    code = code + (mask_ref[order_ref[k], base + first // TILE + p * tiles + t] << k)
                matrix = t_ref[:, pl.ds(pl.multiple_of(code * TILE, TILE), TILE)][:, 0:members]
                y = jnp.dot(matrix, x, precision=HIGHEST, preferred_element_type=jnp.float32)
                for d in range(n_mem):
                    outs[d][rows, at + t * TILE : at + (t + 1) * TILE] = y[d * mem_loc : (d + 1) * mem_loc, :]
        at += width // parts


def on_device(state, obs_tile, obs_offset, obs_value, obs_error, loc_mask, block_order):
    f32 = jnp.float32
    n_mem = lax.axis_size("mem")
    n_grid = lax.axis_size("grid")
    mem_loc, grid_width = state.shape
    members = mem_loc * n_mem
    quarter = grid_width // n_mem
    parts = 8 // math.gcd(mem_loc, 8)
    obs = obs_value.shape[1]
    unit = parts * TILE
    units = quarter // unit
    cuts = [units * cut // 16 * unit for cut in (8,)]
    firsts = [0] + cuts
    widths = [end - first for first, end in zip(firsts, cuts + [quarter])]
    every = tuple(range(len(firsts)))

    def swap(value, axis, by):
        return lax.ppermute(value, axis, [(j, j ^ by) for j in range(lax.axis_size(axis))])

    def pack(jobs, *after):
        chunks = [(d, [(firsts[c], widths[c]) for c in which]) for d, which in jobs]
        total = [sum(width for _, width in each) for _, each in chunks]
        return kernel_call(
            functools.partial(pack_kernel, parts, quarter, chunks),
            "pack",
            [jax.ShapeDtypeStruct((parts * mem_loc, width // parts), f32) for width in total],
            [VMEM] + [ANY] * len(after),
            [VMEM] * len(jobs),
        )(state, *after)

    def update_matrices(slab):
        hop = 1
        while True:
            other = swap(slab, "grid", hop)
            hop *= 2
            if hop >= n_grid:
                break
            slab = slab + other
        return kernel_call(
            functools.partial(chain_kernel, places),
            "chain",
            jax.ShapeDtypeStruct((members, TILE << BLOCKS), f32),
            [SMEM] * 3 + [VMEM] * 5,
            VMEM,
            [pltpu.VMEM((BLOCKS, members, TILE), f32), pltpu.VMEM((TILE, obs), f32)],
        )(obs_tile, block_order, loc_mask, obs_offset, obs_value, obs_error, slab, other)

    def no_updates(slab):
        return jnp.tile(jnp.eye(members, TILE, dtype=f32), (1, 1 << BLOCKS))

    mine = kernel_call(
        seen_kernel,
        "seen",
        jax.ShapeDtypeStruct((BLOCKS * mem_loc, TILE), f32),
        [HBM, HBM, VMEM],
        VMEM,
        [
            pltpu.SMEM((BLOCKS,), jnp.int32),
            pltpu.SMEM((BLOCKS,), jnp.int32),
            pltpu.SemaphoreType.DMA((2,)),
        ],
    )(obs_tile, block_order, state)
    places = range(n_mem)
    seen = [mine] + [swap(mine, "mem", d) for d in places[1:]]
    held = {}

    def start(jobs, *after):
        for job, value in zip(jobs, pack(jobs, *after)):
            held[job] = swap(value, "mem", job[0]) if job[0] else value

    last = n_mem - 1

    start([(d, every) for d in range(last)] + [(last, (0,)), (last, (1,))], *seen)

    slab = kernel_call(
        functools.partial(join_kernel, n_mem),
        "join",
        jax.ShapeDtypeStruct((n_mem * BLOCKS * mem_loc, TILE), f32),
        [VMEM] * n_mem,
        VMEM,
    )(*seen)
    matrices = lax.cond(jnp.any(loc_mask > 0), update_matrices, no_updates, slab)
    result = []
    for group in ((0,), (1,)):
        jobs = sorted({job for job in held if set(job[1]) & set(group)})
        chunks = []
        for c in group:
            sources = []
            for d in range(n_mem):
                job = next(job for job in jobs if job[0] == d and c in job[1])
                sources.append((jobs.index(job), sum(widths[b] for b in job[1] if b < c) // parts))
            chunks.append((firsts[c], widths[c], sources))
        total = sum(widths[c] for c in group)
        updated = kernel_call(
            functools.partial(apply_kernel, n_mem, parts, quarter, chunks),
            "apply",
            [jax.ShapeDtypeStruct((parts * mem_loc, total // parts), f32)] * n_mem,
            [SMEM] * 2 + [VMEM] * (1 + len(jobs)),
            [VMEM] * n_mem,
        )(block_order, loc_mask, matrices, *[held[job] for job in jobs])
        back = [updated[0]] + [swap(updated[d], "mem", d) for d in range(1, n_mem)]
        for shifts in (range(2), range(2, n_mem)):
            result = kernel_call(
                functools.partial(unpack_kernel, parts, quarter, [chunk[:2] for chunk in chunks], shifts),
                "unpack",
                [jax.ShapeDtypeStruct(state.shape, f32)],
                [VMEM] * len(shifts) + [HBM] * len(result),
                [HBM],
                [pltpu.VMEM((len(shifts), mem_loc, total), f32), pltpu.SemaphoreType.DMA((len(shifts),))],
                {len(shifts): 0} if result else None,
            )(*[back[d] for d in shifts], *result)
    return result[0]


def solution(mesh):
    placed = (P("mem", "grid"), P(), P(), P(), P(), P(), P())
    return jax.shard_map(
        on_device, mesh=mesh, in_specs=placed, out_specs=P("mem", "grid"), check_vma=False
    )
```

```python
import functools
import math

import jax
import jax.numpy as jnp
from jax import lax
from jax.experimental import pallas as pl
from jax.experimental.pallas import tpu as pltpu
from jax.sharding import PartitionSpec as P

BLOCKS = 4
TILE = 128
HIGHEST = lax.Precision.HIGHEST
VMEM = pl.BlockSpec(memory_space=pltpu.VMEM)
SMEM = pl.BlockSpec(memory_space=pltpu.SMEM)
ANY = pl.BlockSpec(memory_space=pl.ANY)
HBM = pl.BlockSpec(memory_space=pltpu.HBM)


def kernel_call(kernel, name, out_shape, in_specs, out_specs, scratch_shapes=(), aliases=None, vmem=12):
    return pl.pallas_call(
        kernel,
        name=name,
        out_shape=out_shape,
        in_specs=in_specs,
        out_specs=out_specs,
        scratch_shapes=scratch_shapes,
        input_output_aliases=aliases or {},
        compiler_params=pltpu.CompilerParams(vmem_limit_bytes=vmem << 20),
    )


def run_all(copies):
    for copy in copies:
        copy.start()
    for copy in copies:
        copy.wait()


def seen_kernel(tile_ref, order_ref, x_ref, out, tile, order, sem):
    mem_loc, grid_width = x_ref.shape
    tiles_here = grid_width // TILE
    run_all(
        [
            pltpu.make_async_copy(tile_ref, tile, sem.at[0]),
            pltpu.make_async_copy(order_ref, order, sem.at[1]),
        ]
    )
    for k in range(BLOCKS):
        at = tile[order[k]]
        cols = pl.ds(pl.multiple_of(lax.rem(at, tiles_here) * TILE, TILE), TILE)
        here = at // tiles_here == lax.axis_index("grid")
        out[k * mem_loc : (k + 1) * mem_loc, :] = jnp.where(here, x_ref[:, cols], 0.0)


def piece_columns(d, quarter, first, width):
    return pl.ds(pl.multiple_of((lax.axis_index("mem") ^ d) * quarter + first, TILE), width)


def pack_kernel(parts, quarter, jobs, x_ref, *refs):
    outs = refs[-len(jobs) :]
    mem_loc = x_ref.shape[0]
    for (d, chunks), out in zip(jobs, outs):
        to = 0
        for first, width in chunks:
            width = width // parts
            for p in range(parts):
                cols = piece_columns(d, quarter, first + p * width, width)
                out[p * mem_loc : (p + 1) * mem_loc, to : to + width] = x_ref[:, cols]
            to += width


def unpack_kernel(parts, quarter, chunks, shifts, *refs):
    out, held, sem = refs[-3:]
    mem_loc = out.shape[0]
    copies = []
    for i, d in enumerate(shifts):
        at = 0
        for first, width in chunks:
            side = width // parts
            for p in range(parts):
                part = refs[i][p * mem_loc : (p + 1) * mem_loc, at // parts : at // parts + side]
                held[i, :, at + p * side : at + (p + 1) * side] = part
            at += width
        first, total = chunks[0][0], sum(width for _, width in chunks)
        copies.append(
            pltpu.make_async_copy(held.at[i], out.at[:, piece_columns(d, quarter, first, total)], sem.at[i])
        )
        copies[i].start()
    for copy in copies:
        copy.wait()


def join_kernel(count, *refs):
    rows = refs[0].shape[0]
    for i in range(count):
        refs[-1][i * rows : (i + 1) * rows, :] = refs[i][...]


def chain_kernel(
    places, tile_ref, order_ref, mask_ref, offset_ref, value_ref, error_ref, one_ref, two_ref, out, slab, rows_ref
):
    members = slab.shape[1]
    mem_loc = members // len(places)
    obs = offset_ref.shape[1]
    for k in range(BLOCKS):
        for i, ref in enumerate((offset_ref, value_ref, error_ref)):
            rows_ref[3 * k + i : 3 * k + i + 1, :] = ref[pl.ds(order_ref[k], 1), :].astype(jnp.float32)
    columns = jnp.transpose(rows_ref[...])
    for i, d in enumerate(places):
        for k in range(BLOCKS):
            rows = slice((i * BLOCKS + k) * mem_loc, (i * BLOCKS + k + 1) * mem_loc)
            slab[k, d * mem_loc : (d + 1) * mem_loc, :] = one_ref[rows, :] + two_ref[rows, :]
    row = lax.broadcasted_iota(jnp.int32, (members, TILE), 0)
    lane = lax.broadcasted_iota(jnp.int32, (members, TILE), 1)
    out[:, 0:TILE] = jnp.where(row == lane, 1.0, 0.0)
    place = lax.broadcasted_iota(jnp.int32, (obs, TILE), 1).astype(jnp.float32)
    for k in range(BLOCKS):
        x = slab[k]
        ybar = jnp.sum(x, axis=0, keepdims=True) / members
        dev = x - ybar
        var = jnp.sum(dev * dev, axis=0, keepdims=True) / (members - 1.0)
        offset, value, error = (columns[:, 3 * k + i : 3 * k + i + 1] for i in range(3))
        hit = offset == place
        total = var + error
        shrink = jnp.where(hit, jnp.sqrt(error / total) - 1.0, 0.0)
        shift = jnp.where(hit, var / total * (value - ybar), 0.0)
        scale = 1.0 / ((members - 1.0) * (var + 1e-05))
        shrink = jnp.sum(shrink, axis=0, keepdims=True) * scale
        shift = jnp.sum(shift, axis=0, keepdims=True) * scale
        centred = dev - jnp.sum(dev, axis=0, keepdims=True) / members
        gain = lax.dot_general(
            dev * shrink + shift,
            centred,
            (((1,), (1,)), ((), ())),
            precision=HIGHEST,
            preferred_element_type=jnp.float32,
        )
        for j in range(k + 1, BLOCKS):
            old = slab[j]
            new = old + jnp.dot(gain, old, precision=HIGHEST, preferred_element_type=jnp.float32)
            used = mask_ref[order_ref[k], tile_ref[order_ref[j]]]
            slab[j] = jnp.where(used == 1, new, old)
        span = TILE << k
        so_far = out[:, 0:span]
        out[:, span : 2 * span] = so_far + jnp.dot(
            gain, so_far, precision=HIGHEST, preferred_element_type=jnp.float32
        )


def apply_kernel(n_mem, parts, quarter, chunks, order_ref, mask_ref, t_ref, *refs):
    refs, outs = refs[:-n_mem], refs[-n_mem:]
    mem_loc = outs[0].shape[0] // parts
    members = mem_loc * n_mem
    base = (lax.axis_index("grid") * n_mem + lax.axis_index("mem")) * (quarter // TILE)
    at = 0
    for first, width, sources in chunks:
        tiles = width // parts // TILE
        for p in range(parts):
            rows = slice(p * mem_loc, (p + 1) * mem_loc)
            for t in range(tiles):
                x = jnp.concatenate(
                    [refs[i][rows, start + t * TILE : start + (t + 1) * TILE] for i, start in sources], axis=0
                )
                code = 0
                for k in range(BLOCKS):
                    code = code + (mask_ref[order_ref[k], base + first // TILE + p * tiles + t] << k)
                matrix = t_ref[:, pl.ds(pl.multiple_of(code * TILE, TILE), TILE)][:, 0:members]
                y = jnp.dot(matrix, x, precision=HIGHEST, preferred_element_type=jnp.float32)
                for d in range(n_mem):
                    outs[d][rows, at + t * TILE : at + (t + 1) * TILE] = y[d * mem_loc : (d + 1) * mem_loc, :]
        at += width // parts


def on_device(state, obs_tile, obs_offset, obs_value, obs_error, loc_mask, block_order):
    f32 = jnp.float32
    n_mem = lax.axis_size("mem")
    n_grid = lax.axis_size("grid")
    mem_loc, grid_width = state.shape
    members = mem_loc * n_mem
    quarter = grid_width // n_mem
    parts = 8 // math.gcd(mem_loc, 8)
    obs = obs_value.shape[1]
    unit = parts * TILE
    units = quarter // unit
    cuts = [units * cut // 16 * unit for cut in (8,)]
    firsts = [0] + cuts
    widths = [end - first for first, end in zip(firsts, cuts + [quarter])]
    every = tuple(range(len(firsts)))

    def swap(value, axis, by):
        return lax.ppermute(value, axis, [(j, j ^ by) for j in range(lax.axis_size(axis))])

    def pack(jobs, *after):
        chunks = [(d, [(firsts[c], widths[c]) for c in which]) for d, which in jobs]
        total = [sum(width for _, width in each) for _, each in chunks]
        return kernel_call(
            functools.partial(pack_kernel, parts, quarter, chunks),
            "pack",
            [jax.ShapeDtypeStruct((parts * mem_loc, width // parts), f32) for width in total],
            [VMEM] + [ANY] * len(after),
            [VMEM] * len(jobs),
        )(state, *after)

    def update_matrices(slab):
        hop = 1
        while True:
            other = swap(slab, "grid", hop)
            hop *= 2
            if hop >= n_grid:
                break
            slab = slab + other
        return kernel_call(
            functools.partial(chain_kernel, places),
            "chain",
            jax.ShapeDtypeStruct((members, TILE << BLOCKS), f32),
            [SMEM] * 3 + [VMEM] * 5,
            VMEM,
            [pltpu.VMEM((BLOCKS, members, TILE), f32), pltpu.VMEM((TILE, obs), f32)],
        )(obs_tile, block_order, loc_mask, obs_offset, obs_value, obs_error, slab, other)

    def no_updates(slab):
        return jnp.tile(jnp.eye(members, TILE, dtype=f32), (1, 1 << BLOCKS))

    mine = kernel_call(
        seen_kernel,
        "seen",
        jax.ShapeDtypeStruct((BLOCKS * mem_loc, TILE), f32),
        [HBM, HBM, VMEM],
        VMEM,
        [
            pltpu.SMEM((BLOCKS,), jnp.int32),
            pltpu.SMEM((BLOCKS,), jnp.int32),
            pltpu.SemaphoreType.DMA((2,)),
        ],
    )(obs_tile, block_order, state)
    places = range(n_mem)
    seen = [mine] + [swap(mine, "mem", d) for d in places[1:]]
    held = {}

    def start(jobs, *after):
        for job, value in zip(jobs, pack(jobs, *after)):
            held[job] = swap(value, "mem", job[0]) if job[0] else value

    last = n_mem - 1

    start([(d, every) for d in range(last)] + [(last, (0,)), (last, (1,))], *seen)

    slab = kernel_call(
        functools.partial(join_kernel, n_mem),
        "join",
        jax.ShapeDtypeStruct((n_mem * BLOCKS * mem_loc, TILE), f32),
        [VMEM] * n_mem,
        VMEM,
    )(*seen)
    matrices = lax.cond(jnp.any(loc_mask > 0), update_matrices, no_updates, slab)
    result = []
    for group in ((0,), (1,)):
        jobs = sorted({job for job in held if set(job[1]) & set(group)})
        chunks = []
        for c in group:
            sources = []
            for d in range(n_mem):
                job = next(job for job in jobs if job[0] == d and c in job[1])
                sources.append((jobs.index(job), sum(widths[b] for b in job[1] if b < c) // parts))
            chunks.append((firsts[c], widths[c], sources))
        total = sum(widths[c] for c in group)
        updated = kernel_call(
            functools.partial(apply_kernel, n_mem, parts, quarter, chunks),
            "apply",
            [jax.ShapeDtypeStruct((parts * mem_loc, total // parts), f32)] * n_mem,
            [SMEM] * 2 + [VMEM] * (1 + len(jobs)),
            [VMEM] * n_mem,
        )(block_order, loc_mask, matrices, *[held[job] for job in jobs])
        back = [updated[0]] + [swap(updated[d], "mem", d) for d in range(n_mem - 1, 0, -1)][::-1]
        for shifts in (range(2), range(2, n_mem)):
            result = kernel_call(
                functools.partial(unpack_kernel, parts, quarter, [chunk[:2] for chunk in chunks], shifts),
                "unpack",
                [jax.ShapeDtypeStruct(state.shape, f32)],
                [VMEM] * len(shifts) + [HBM] * len(result),
                [HBM],
                [pltpu.VMEM((len(shifts), mem_loc, total), f32), pltpu.SemaphoreType.DMA((len(shifts),))],
                {len(shifts): 0} if result else None,
            )(*[back[d] for d in shifts], *result)
    return result[0]


def solution(mesh):
    placed = (P("mem", "grid"), P(), P(), P(), P(), P(), P())
    return jax.shard_map(
        on_device, mesh=mesh, in_specs=placed, out_specs=P("mem", "grid"), check_vma=False
    )
```

```python
import functools
import math

import jax
import jax.numpy as jnp
from jax import lax
from jax.experimental import pallas as pl
from jax.experimental.pallas import tpu as pltpu
from jax.sharding import PartitionSpec as P

BLOCKS = 4
TILE = 128
HIGHEST = lax.Precision.HIGHEST
VMEM = pl.BlockSpec(memory_space=pltpu.VMEM)
SMEM = pl.BlockSpec(memory_space=pltpu.SMEM)
ANY = pl.BlockSpec(memory_space=pl.ANY)
HBM = pl.BlockSpec(memory_space=pltpu.HBM)


def kernel_call(kernel, name, out_shape, in_specs, out_specs, scratch_shapes=(), aliases=None, vmem=12):
    return pl.pallas_call(
        kernel,
        name=name,
        out_shape=out_shape,
        in_specs=in_specs,
        out_specs=out_specs,
        scratch_shapes=scratch_shapes,
        input_output_aliases=aliases or {},
        compiler_params=pltpu.CompilerParams(vmem_limit_bytes=vmem << 20),
    )


def run_all(copies):
    for copy in copies:
        copy.start()
    for copy in copies:
        copy.wait()


def seen_kernel(tile_ref, order_ref, x_ref, out, tile, order, sem):
    mem_loc, grid_width = x_ref.shape
    tiles_here = grid_width // TILE
    run_all(
        [
            pltpu.make_async_copy(tile_ref, tile, sem.at[0]),
            pltpu.make_async_copy(order_ref, order, sem.at[1]),
        ]
    )
    for k in range(BLOCKS):
        at = tile[order[k]]
        cols = pl.ds(pl.multiple_of(lax.rem(at, tiles_here) * TILE, TILE), TILE)
        here = at // tiles_here == lax.axis_index("grid")
        out[k * mem_loc : (k + 1) * mem_loc, :] = jnp.where(here, x_ref[:, cols], 0.0)


def piece_columns(d, quarter, first, width):
    return pl.ds(pl.multiple_of((lax.axis_index("mem") ^ d) * quarter + first, TILE), width)


def pack_kernel(parts, quarter, jobs, x_ref, *refs):
    outs = refs[-len(jobs) :]
    mem_loc = x_ref.shape[0]
    for (d, chunks), out in zip(jobs, outs):
        to = 0
        for first, width in chunks:
            width = width // parts
            for p in range(parts):
                cols = piece_columns(d, quarter, first + p * width, width)
                out[p * mem_loc : (p + 1) * mem_loc, to : to + width] = x_ref[:, cols]
            to += width


def unpack_kernel(parts, quarter, chunks, shifts, *refs):
    out, held, sem = refs[-3:]
    mem_loc = out.shape[0]
    copies = []
    for i, d in enumerate(shifts):
        at = 0
        for first, width in chunks:
            side = width // parts
            for p in range(parts):
                part = refs[i][p * mem_loc : (p + 1) * mem_loc, at // parts : at // parts + side]
                held[i, :, at + p * side : at + (p + 1) * side] = part
            at += width
        first, total = chunks[0][0], sum(width for _, width in chunks)
        copies.append(
            pltpu.make_async_copy(held.at[i], out.at[:, piece_columns(d, quarter, first, total)], sem.at[i])
        )
        copies[i].start()
    for copy in copies:
        copy.wait()


def join_kernel(count, *refs):
    rows = refs[0].shape[0]
    for i in range(count):
        refs[-1][i * rows : (i + 1) * rows, :] = refs[i][...]


def chain_kernel(
    places, tile_ref, order_ref, mask_ref, offset_ref, value_ref, error_ref, one_ref, two_ref, out, slab, rows_ref
):
    members = slab.shape[1]
    mem_loc = members // len(places)
    obs = offset_ref.shape[1]
    for k in range(BLOCKS):
        for i, ref in enumerate((offset_ref, value_ref, error_ref)):
            rows_ref[3 * k + i : 3 * k + i + 1, :] = ref[pl.ds(order_ref[k], 1), :].astype(jnp.float32)
    columns = jnp.transpose(rows_ref[...])
    for i, d in enumerate(places):
        for k in range(BLOCKS):
            rows = slice((i * BLOCKS + k) * mem_loc, (i * BLOCKS + k + 1) * mem_loc)
            slab[k, d * mem_loc : (d + 1) * mem_loc, :] = one_ref[rows, :] + two_ref[rows, :]
    row = lax.broadcasted_iota(jnp.int32, (members, TILE), 0)
    lane = lax.broadcasted_iota(jnp.int32, (members, TILE), 1)
    out[:, 0:TILE] = jnp.where(row == lane, 1.0, 0.0)
    place = lax.broadcasted_iota(jnp.int32, (obs, TILE), 1).astype(jnp.float32)
    for k in range(BLOCKS):
        x = slab[k]
        ybar = jnp.sum(x, axis=0, keepdims=True) / members
        dev = x - ybar
        var = jnp.sum(dev * dev, axis=0, keepdims=True) / (members - 1.0)
        offset, value, error = (columns[:, 3 * k + i : 3 * k + i + 1] for i in range(3))
        hit = offset == place
        total = var + error
        shrink = jnp.where(hit, jnp.sqrt(error / total) - 1.0, 0.0)
        shift = jnp.where(hit, var / total * (value - ybar), 0.0)
        scale = 1.0 / ((members - 1.0) * (var + 1e-05))
        shrink = jnp.sum(shrink, axis=0, keepdims=True) * scale
        shift = jnp.sum(shift, axis=0, keepdims=True) * scale
        centred = dev - jnp.sum(dev, axis=0, keepdims=True) / members
        gain = lax.dot_general(
            dev * shrink + shift,
            centred,
            (((1,), (1,)), ((), ())),
            precision=HIGHEST,
            preferred_element_type=jnp.float32,
        )
        for j in range(k + 1, BLOCKS):
            old = slab[j]
            new = old + jnp.dot(gain, old, precision=HIGHEST, preferred_element_type=jnp.float32)
            used = mask_ref[order_ref[k], tile_ref[order_ref[j]]]
            slab[j] = jnp.where(used == 1, new, old)
        span = TILE << k
        so_far = out[:, 0:span]
        out[:, span : 2 * span] = so_far + jnp.dot(
            gain, so_far, precision=HIGHEST, preferred_element_type=jnp.float32
        )


def apply_kernel(n_mem, parts, quarter, chunks, order_ref, mask_ref, t_ref, *refs):
    refs, outs = refs[:-n_mem], refs[-n_mem:]
    mem_loc = outs[0].shape[0] // parts
    members = mem_loc * n_mem
    base = (lax.axis_index("grid") * n_mem + lax.axis_index("mem")) * (quarter // TILE)
    at = 0
    for first, width, sources in chunks:
        tiles = width // parts // TILE
        for p in range(parts):
            rows = slice(p * mem_loc, (p + 1) * mem_loc)
            for t in range(tiles):
                x = jnp.concatenate(
                    [refs[i][rows, start + t * TILE : start + (t + 1) * TILE] for i, start in sources], axis=0
                )
                code = 0
                for k in range(BLOCKS):
                    code = code + (mask_ref[order_ref[k], base + first // TILE + p * tiles + t] << k)
                matrix = t_ref[:, pl.ds(pl.multiple_of(code * TILE, TILE), TILE)][:, 0:members]
                y = jnp.dot(matrix, x, precision=HIGHEST, preferred_element_type=jnp.float32)
                for d in range(n_mem):
                    outs[d][rows, at + t * TILE : at + (t + 1) * TILE] = y[d * mem_loc : (d + 1) * mem_loc, :]
        at += width // parts


def on_device(state, obs_tile, obs_offset, obs_value, obs_error, loc_mask, block_order):
    f32 = jnp.float32
    n_mem = lax.axis_size("mem")
    n_grid = lax.axis_size("grid")
    mem_loc, grid_width = state.shape
    members = mem_loc * n_mem
    quarter = grid_width // n_mem
    parts = 8 // math.gcd(mem_loc, 8)
    obs = obs_value.shape[1]
    unit = parts * TILE
    units = quarter // unit
    cuts = [units * cut // 16 * unit for cut in (8,)]
    firsts = [0] + cuts
    widths = [end - first for first, end in zip(firsts, cuts + [quarter])]
    every = tuple(range(len(firsts)))

    def swap(value, axis, by):
        return lax.ppermute(value, axis, [(j, j ^ by) for j in range(lax.axis_size(axis))])

    def pack(jobs, *after):
        chunks = [(d, [(firsts[c], widths[c]) for c in which]) for d, which in jobs]
        total = [sum(width for _, width in each) for _, each in chunks]
        return kernel_call(
            functools.partial(pack_kernel, parts, quarter, chunks),
            "pack",
            [jax.ShapeDtypeStruct((parts * mem_loc, width // parts), f32) for width in total],
            [VMEM] + [ANY] * len(after),
            [VMEM] * len(jobs),
        )(state, *after)

    def update_matrices(slab):
        hop = 2
        while True:
            other = swap(slab, "grid", hop)
            hop *= 2
            if hop >= n_grid:
                break
            slab = slab + other
        return kernel_call(
            functools.partial(chain_kernel, places),
            "chain",
            jax.ShapeDtypeStruct((members, TILE << BLOCKS), f32),
            [SMEM] * 3 + [VMEM] * 5,
            VMEM,
            [pltpu.VMEM((BLOCKS, members, TILE), f32), pltpu.VMEM((TILE, obs), f32)],
        )(obs_tile, block_order, loc_mask, obs_offset, obs_value, obs_error, slab, other)

    def no_updates(slab):
        return jnp.tile(jnp.eye(members, TILE, dtype=f32), (1, 1 << BLOCKS))

    mine = kernel_call(
        seen_kernel,
        "seen",
        jax.ShapeDtypeStruct((BLOCKS * mem_loc, TILE), f32),
        [HBM, HBM, VMEM],
        VMEM,
        [
            pltpu.SMEM((BLOCKS,), jnp.int32),
            pltpu.SMEM((BLOCKS,), jnp.int32),
            pltpu.SemaphoreType.DMA((2,)),
        ],
    )(obs_tile, block_order, state)
    places = range(n_mem)
    seen = [mine] + [swap(mine, "mem", d) for d in places[1:]]
    held = {}

    def start(jobs, *after):
        for job, value in zip(jobs, pack(jobs, *after)):
            held[job] = swap(value, "mem", job[0]) if job[0] else value

    last = n_mem - 1

    start([(d, every) for d in range(last)] + [(last, (0,)), (last, (1,))], *seen)

    slab = kernel_call(
        functools.partial(join_kernel, n_mem),
        "join",
        jax.ShapeDtypeStruct((n_mem * BLOCKS * mem_loc, TILE), f32),
        [VMEM] * n_mem,
        VMEM,
    )(*seen)
    slab = slab + swap(slab, "grid", 1)
    matrices = lax.cond(jnp.any(loc_mask > 0), update_matrices, no_updates, slab)
    result = []
    for group in ((0,), (1,)):
        jobs = sorted({job for job in held if set(job[1]) & set(group)})
        chunks = []
        for c in group:
            sources = []
            for d in range(n_mem):
                job = next(job for job in jobs if job[0] == d and c in job[1])
                sources.append((jobs.index(job), sum(widths[b] for b in job[1] if b < c) // parts))
            chunks.append((firsts[c], widths[c], sources))
        total = sum(widths[c] for c in group)
        updated = kernel_call(
            functools.partial(apply_kernel, n_mem, parts, quarter, chunks),
            "apply",
            [jax.ShapeDtypeStruct((parts * mem_loc, total // parts), f32)] * n_mem,
            [SMEM] * 2 + [VMEM] * (1 + len(jobs)),
            [VMEM] * n_mem,
        )(block_order, loc_mask, matrices, *[held[job] for job in jobs])
        back = [updated[0]] + [swap(updated[d], "mem", d) for d in range(n_mem - 1, 0, -1)][::-1]
        for shifts in (range(2), range(2, n_mem)):
            result = kernel_call(
                functools.partial(unpack_kernel, parts, quarter, [chunk[:2] for chunk in chunks], shifts),
                "unpack",
                [jax.ShapeDtypeStruct(state.shape, f32)],
                [VMEM] * len(shifts) + [HBM] * len(result),
                [HBM],
                [pltpu.VMEM((len(shifts), mem_loc, total), f32), pltpu.SemaphoreType.DMA((len(shifts),))],
                {len(shifts): 0} if result else None,
            )(*[back[d] for d in shifts], *result)
    return result[0]


def solution(mesh):
    placed = (P("mem", "grid"), P(), P(), P(), P(), P(), P())
    return jax.shard_map(
        on_device, mesh=mesh, in_specs=placed, out_specs=P("mem", "grid"), check_vma=False
    )
```
